32 devices in a mesh: ep: 8 (over z, y), tp: 4 (over x, core).
Axes of the slice: x: 2, y: 2, z: 4, core: 2. Of those that a mesh axis runs over, the one named last changes fastest.
Arguments:
- tokens: bfloat16 [2048, 3584], P('ep', 'tp'), may hold values from -6 to 6
- expert_ids: int32 [2048, 8], P('ep'), may hold values from 0 to 255, as said below
- gate_weight: bfloat16 [8, 3584, 2048], P('ep', None, 'tp'), may hold values from -0.09375 to 0.09375
- up_weight: bfloat16 [8, 3584, 2048], P('ep', None, 'tp'), may hold values from -0.09375 to 0.09375
Outputs:
- hidden: bfloat16 [8, 128, 2048], P('ep', None, 'tp')
- hessian: float32 [8, 2048, 2048], P('ep', 'tp')
The draws below stay inside these ranges and needn't reach their ends.
Inputs may be any that keep to these rules, and one draw needn't show every extreme that they name: `expert_ids`: each row names 8 different experts. In the rows of one source block (one index of ep) every expert id appears 0, 8 or 16 times, and some expert id below 8 appears exactly 16 times in every source block.
All inputs are finite; a program needn't handle non-finite values.
Results may differ from the reference program's by a relative error of at most 0.0045.
Values may be sent and summed in bfloat16 or wider, within the bound.
No kernel may reach another device: no remote copies, remote signals or barrier semaphores. Data moves between devices by JAX's collectives and lax.ppermute only.
A program may use at most 64 MiB of HBM per device.

```python
import jax
import jax.numpy as jnp
from jax import lax

D = 3584
FF = 2048
EXPERTS = 256
TOP = 8
TOK_DEV = 256
TOKENS = 2048
CAP = 16
SLOTS = 128
N_EP = 8


def draw_expert_ids(key, part):
    quarter = EXPERTS // 4
    forced = jax.random.randint(jax.random.fold_in(key, 7), (), 0, N_EP)
    positions = jnp.arange(EXPERTS)

    def one_block(block_key):
        key_one, key_two, key_three = jax.random.split(block_key, 3)
        shuffled = jax.random.permutation(key_one, EXPERTS)
        spot_index = jax.random.randint(key_two, (), 0, quarter)
        where_forced = jnp.argmax(shuffled == forced)
        at_spot = shuffled[spot_index]
        shuffled = jnp.where(positions == where_forced, at_spot, shuffled)
        shuffled = jnp.where(positions == spot_index, forced, shuffled)
        offset = jax.random.randint(key_three, (), 0, EXPERTS)
        table_index = jnp.where(positions < 2 * quarter, positions, jnp.where(positions < 3 * quarter, positions - 2 * quarter, positions - quarter))
        lookup = shuffled[table_index]
        route_pos = jnp.arange(TOK_DEV)[:, None] * TOP + jnp.arange(TOP)[None, :]
        return lookup[(route_pos + offset) % EXPERTS]
    block_keys = jax.vmap(lambda number: jax.random.fold_in(key, number))(jnp.arange(N_EP) + 100)
    return jax.vmap(one_block)(block_keys).reshape(TOKENS, TOP).astype(jnp.int32)


def level_of(own_key, shape, pieces, least, largest):
    loudness, own = 1.0, jax.random.fold_in(own_key, 6)
    for position, blocks in pieces:
        draws = jnp.exp(jax.random.uniform(jax.random.fold_in(own, position), (blocks,), jnp.float32, least / len(pieces), largest / len(pieces)))
        loudness = loudness * jnp.repeat(draws, shape[position] // blocks).reshape([-1 if axis == position else 1 for axis in range(len(shape))])
    return loudness


def bell_draw(stream_key, extent, deviation, limit, cuts=(), kind=jnp.bfloat16):
    result = deviation * jax.random.normal(stream_key, extent, jnp.float32)
    if cuts:
        result = result * level_of(stream_key, extent, cuts, -0.22, 0.18)
    return jnp.clip(result, -limit, limit).astype(kind)


def setup_inputs(seed: int = 0) -> dict:
    key_list = jax.random.split(jax.random.key(seed), 5)
    tokens = bell_draw(key_list[0], (TOKENS, D), 1.0, 6.0, ((0, 8), (1, 4)))
    expert_ids = draw_expert_ids(jax.random.fold_in(key_list[4], 71), 0)
    gate_weight = bell_draw(key_list[2], (N_EP, D, FF), D ** -0.5, 0.09375, ((0, 8), (2, 4)))
    up_weight = bell_draw(key_list[3], (N_EP, D, FF), D ** -0.5, 0.09375, ((0, 8), (2, 4)))
    return dict(tokens=tokens, expert_ids=expert_ids, gate_weight=gate_weight, up_weight=up_weight)


def one_expert(expert, tokens, expert_ids, gate_weight, up_weight):
    member = jnp.any(expert_ids == expert, axis=1).astype(jnp.int32).reshape(N_EP, TOK_DEV)
    ranking = jnp.cumsum(member, axis=1).astype(jnp.int32) - 1
    source = jnp.arange(N_EP, dtype=jnp.int32)[:, None]
    slot_of = jnp.where(member > 0, source * CAP + ranking, SLOTS).reshape(-1).astype(jnp.int32)
    token_of = jnp.full((SLOTS + 1,), TOKENS, jnp.int32).at[slot_of].set(jnp.arange(TOKENS, dtype=jnp.int32))
    token_of = token_of[:SLOTS]
    padded = jnp.concatenate([tokens, jnp.zeros((1, D), tokens.dtype)], axis=0)
    routed = padded[token_of]
    gate_proj = jnp.dot(routed, gate_weight[expert], preferred_element_type=jnp.float32)
    up_proj = jnp.dot(routed, up_weight[expert], preferred_element_type=jnp.float32)
    hidden = (jax.nn.silu(gate_proj) * up_proj).astype(jnp.bfloat16)
    hessian = jnp.dot(hidden.T, hidden, preferred_element_type=jnp.float32) * (2.0 / SLOTS)
    return hidden, hessian


def reference(tokens, expert_ids, gate_weight, up_weight):
    def apply_one(expert):
        return one_expert(expert, tokens, expert_ids, gate_weight, up_weight)

    hidden, hessian = lax.map(apply_one, jnp.arange(N_EP, dtype=jnp.int32))
    return hidden, hessian
```

```python
import functools

import jax
import jax.numpy as jnp
from jax import lax
from jax.experimental import pallas as pl
from jax.experimental.pallas import tpu as pltpu
from jax.sharding import PartitionSpec as P

EXPERTS = 256
TOP = 8
BF16 = jnp.bfloat16
F32 = jnp.float32
VMEM = pl.BlockSpec(memory_space=pltpu.VMEM)
ANY = pl.BlockSpec(memory_space=pl.ANY)
HBM = pl.BlockSpec(memory_space=pltpu.HBM)
LIMIT = 48 * 1024 * 1024


def dot(a, b):
    return lax.dot_general(a, b, (((1,), (0,)), ((), ())), preferred_element_type=F32)


def select_kernel(groups, capacity, ids_hbm, tok_hbm, out_ref, ids_ref, tok_ref, sems):
    get_ids = pltpu.make_async_copy(ids_hbm, ids_ref, sems.at[0])
    get_tok = pltpu.make_async_copy(tok_hbm, tok_ref, sems.at[1])
    get_ids.start()
    get_tok.start()
    rows = ids_ref.shape[1]
    before = lax.broadcasted_iota(jnp.int32, (rows, rows), 0)
    after = lax.broadcasted_iota(jnp.int32, (rows, rows), 1)
    upto = jnp.where(before <= after, 1.0, 0.0).astype(BF16)
    want = lax.broadcasted_iota(jnp.int32, (8, capacity, rows), 1).astype(F32)
    get_ids.wait()
    ids = ids_ref[...]
    for base in range(0, groups, 8):
        expert = base + lax.broadcasted_iota(jnp.int32, (8, rows), 0)
        hit = ids[0:1, :] == expert
        for k in range(1, ids.shape[0]):
            hit = hit | (ids[k : k + 1, :] == expert)
        count = dot(jnp.where(hit, 1.0, 0.0).astype(BF16), upto)
        slot = jnp.where(hit, count - 1.0, -1.0)
        chosen = jnp.where(slot[:, None, :] == want, 1.0, 0.0)
        chosen = chosen.reshape(8 * capacity, rows).astype(BF16)
        if base == 0:
            get_tok.wait()
        out_ref[pl.ds(base * capacity, 8 * capacity), :] = dot(chosen, tok_ref[...]).astype(BF16)


def first_kernel(own_ref, sib_ref, gate_hbm, up_hbm, g_ref, u_ref, rest_ref, wbuf, sems):
    t = lax.axis_index("tp")
    depth = own_ref.shape[1]
    copies = []
    for n, slice_index in enumerate((t, t ^ 1, t ^ 2, t ^ 3)):
        at = pl.ds(pl.multiple_of(slice_index * depth, depth), depth)
        for m, w in enumerate((gate_hbm, up_hbm)):
            target = wbuf.at[n, m] if n < 2 else rest_ref.at[n - 2, m]
            copies.append(pltpu.make_async_copy(w.at[0, at, :], target, sems.at[n * 2 + m]))
    for c in copies:
        c.start()
    for n, block in enumerate((own_ref, sib_ref)):
        for m, total in enumerate((g_ref, u_ref)):
            copies[n * 2 + m].wait()
            part = dot(block[...], wbuf[n, m])
            if n == 0:
                total[...] = part
            else:
                total[...] += part
    for c in copies[4:]:
        c.wait()


def more_kernel(first, x_ref, rest_ref, g_in, u_in, g_ref, u_ref):
    at = pl.ds(first, x_ref.shape[0])
    g_ref[...] = g_in[at, :] + dot(x_ref[...], rest_ref[0, 0])
    u_ref[...] = u_in[at, :] + dot(x_ref[...], rest_ref[0, 1])


def last_kernel(d_ref, rest_ref, g_in, u_in, h_ref):
    gate = g_in[...] + dot(d_ref[...], rest_ref[1, 0])
    up = u_in[...] + dot(d_ref[...], rest_ref[1, 1])
    h_ref[...] = (gate / (1.0 + jnp.exp(-gate)) * up).astype(BF16)


def write_block(flip, h_ref, factor, index, hess_hbm, buf, sems):
    wide = h_ref.shape[1]
    part = wide // 4
    at = pl.ds(pl.multiple_of(index * wide, wide), wide)
    copies = []
    for i in range(4):
        rows = pl.ds(i * part, part)
        buf[rows, :] = dot(flip[rows, :], h_ref[...]) * factor
        copies.append(pltpu.make_async_copy(buf.at[rows, :], hess_hbm.at[0, rows, at], sems.at[i]))
        copies[-1].start()
    return copies


def near_kernel(factor, h_ref, sib_ref, flip_ref, hid_hbm, hess_hbm, buf, sems):
    t = lax.axis_index("tp")
    out = pltpu.make_async_copy(h_ref, hid_hbm.at[0], sems.at[2, 0])
    out.start()
    flip_ref[...] = h_ref[...].astype(F32).T.astype(BF16)
    copies = write_block(flip_ref, h_ref, factor, t, hess_hbm, buf.at[0], sems.at[0])
    copies += write_block(flip_ref, sib_ref, factor, t ^ 1, hess_hbm, buf.at[1], sems.at[1])
    out.wait()
    for c in copies:
        c.wait()


def other_kernel(factor, which, flip_ref, h_ref, hess_in, hess_hbm, buf, sems):
    t = lax.axis_index("tp")
    for c in write_block(flip_ref, h_ref, factor, t ^ which, hess_hbm, buf, sems):
        c.wait()


def call(kernel, out_shape, in_specs, out_specs, scratch=(), name=None, aliases={}, flops=0, moved=0):
    return pl.pallas_call(
        kernel,
        out_shape=out_shape,
        in_specs=in_specs,
        out_specs=out_specs,
        scratch_shapes=list(scratch),
        input_output_aliases=aliases,
        name=name,
        cost_estimate=pl.CostEstimate(flops=flops, bytes_accessed=moved, transcendentals=0),
        compiler_params=pltpu.CompilerParams(vmem_limit_bytes=LIMIT),
    )


def on_device(tokens, expert_ids, gate_weight, up_weight):
    groups = lax.axis_size("ep")
    tok_rows, depth = tokens.shape
    capacity = 2 * tok_rows * TOP // EXPERTS
    slots = groups * capacity
    wide = gate_weight.shape[2]
    full = wide * lax.axis_size("tp")
    S = jax.ShapeDtypeStruct
    D = pltpu.SemaphoreType.DMA
    outgoing = call(
        functools.partial(select_kernel, groups, capacity),
        S((slots, depth), BF16), [HBM, HBM], VMEM,
        (pltpu.VMEM(expert_ids.T.shape, jnp.int32), pltpu.VMEM(tokens.shape, BF16), D((2,))), name="select",
    )(expert_ids.T, tokens)
    own = lax.all_to_all(outgoing, "ep", split_axis=0, concat_axis=0, tiled=True)
    cores = [(i, i ^ 1) for i in range(4)]
    chips = [(i, i ^ 2) for i in range(4)]
    parts = 2
    size = slots // parts
    far = [lax.ppermute(own[i * size : (i + 1) * size], "tp", chips) for i in range(parts)]
    sib = lax.ppermute(own, "tp", cores)
    part = S((slots, wide), F32)
    weights = 4 * depth * wide * 2 * 2
    gate, up, rest = call(
        first_kernel,
        (part, part, pltpu.VMEM((2, 2, depth, wide), BF16)),
        [VMEM, VMEM, HBM, HBM], (VMEM, VMEM, VMEM),
        (pltpu.VMEM((2, 2, depth, wide), BF16), D((8,))), name="first",
        flops=8 * slots * depth * wide, moved=weights,
    )(own, sib, gate_weight, up_weight)
    *far, gate = lax.optimization_barrier((*far, gate))
    hidden = []
    some = S((size, wide), F32)
    for i in range(parts):
        diag = lax.ppermute(far[i], "tp", cores)
        g, u = call(
            functools.partial(more_kernel, i * size), (some, some), [VMEM] * 4, (VMEM, VMEM), name="more",
            flops=4 * slots * depth * wide, moved=weights // 16,
        )(far[i], rest, gate, up)
        hidden.append(call(
            last_kernel, S((size, wide), BF16), [VMEM] * 4, VMEM, name="last",
            flops=4 * slots * depth * wide, moved=weights // 16,
        )(diag, rest, g, u))
    hidden = jnp.concatenate(hidden)
    factor = 2.0 / slots
    hess_shape = S((1, wide, full), F32)
    far_h = lax.ppermute(hidden, "tp", chips)
    sib_h = lax.ppermute(hidden, "tp", cores)
    block = wide * wide * 4
    flip, hidden, hess = call(
        functools.partial(near_kernel, factor), (S((wide, slots), BF16), S((1, slots, wide), BF16), hess_shape),
        [VMEM, VMEM], (VMEM, ANY, ANY), (pltpu.VMEM((2, wide, wide), F32), D((3, 4))), name="near",
        flops=4 * slots * wide * wide, moved=2 * block,
    )(hidden, sib_h)

    def other(which, h, hess):
        return call(
            functools.partial(other_kernel, factor, which), hess_shape,
            [VMEM, VMEM, ANY], ANY, (pltpu.VMEM((wide, wide), F32), D((4,))), name="block_%d" % which, aliases={2: 0},
            flops=2 * slots * wide * wide, moved=block,
        )(flip, h, hess)

    far_h, flip = lax.optimization_barrier((far_h, flip))
    diag_h = lax.ppermute(far_h, "tp", cores)
    hess = other(2, far_h, hess)
    hess = other(3, diag_h, hess)
    return hidden, hess


def solution(mesh):
    return jax.shard_map(
        on_device,
        mesh=mesh,
        in_specs=(P("ep", "tp"), P("ep", None), P("ep", None, "tp"), P("ep", None, "tp")),
        out_specs=(P("ep", None, "tp"), P("ep", "tp", None)),
        check_vma=False,
    )
```

```python
import functools

import jax
import jax.numpy as jnp
from jax import lax
from jax.experimental import pallas as pl
from jax.experimental.pallas import tpu as pltpu
from jax.sharding import PartitionSpec as P

EXPERTS = 256
TOP = 8
BF16 = jnp.bfloat16
F32 = jnp.float32
VMEM = pl.BlockSpec(memory_space=pltpu.VMEM)
ANY = pl.BlockSpec(memory_space=pl.ANY)
HBM = pl.BlockSpec(memory_space=pltpu.HBM)
LIMIT = 40 * 1024 * 1024


def dot(a, b):
    return lax.dot_general(a, b, (((1,), (0,)), ((), ())), preferred_element_type=F32)


def weight_copies(gate_hbm, up_hbm, w_ref, sems, chip):
    depth = w_ref.shape[1]
    at = pl.ds(pl.multiple_of(((lax.axis_index("tp") >> 1) ^ chip) * depth, depth), depth)
    return [pltpu.make_async_copy(w.at[0, at, :], w_ref.at[i], sems.at[2 + i]) for i, w in enumerate((gate_hbm, up_hbm))]


def prepare_kernel(capacity, ids_hbm, tok_hbm, gate_hbm, up_hbm, pick_ref, mine_ref, w_ref, ids_ref, tok_ref, sems):
    get = [
        pltpu.make_async_copy(ids_hbm, ids_ref, sems.at[0]),
        pltpu.make_async_copy(tok_hbm, tok_ref, sems.at[1]),
    ] + weight_copies(gate_hbm, up_hbm, w_ref, sems, 0)
    for g in get:
        g.start()
    rows = ids_ref.shape[1]
    before = lax.broadcasted_iota(jnp.int32, (rows, rows), 0)
    after = lax.broadcasted_iota(jnp.int32, (rows, rows), 1)
    upto = jnp.where(before <= after, 1.0, 0.0).astype(BF16)
    want = lax.broadcasted_iota(jnp.int32, (4, capacity, rows), 1).astype(F32)
    core = lax.axis_index("tp") & 1
    step = lax.broadcasted_iota(jnp.int32, (8, rows), 0)
    offset = 2 * step + (core ^ (step & 1))
    expert = lax.axis_index("ep") ^ offset
    get[0].wait()
    ids = ids_ref[...]
    hit = ids[0:1, :] == expert
    for k in range(1, ids.shape[0]):
        hit = hit | (ids[k : k + 1, :] == expert)
    count = dot(jnp.where(hit, 1.0, 0.0).astype(BF16), upto)
    slot = jnp.where(hit, count - 1.0, -1.0)[:4]
    pick = jnp.where(slot[:, None, :] == want, 1.0, 0.0)
    pick = pick.reshape(4 * capacity, rows).astype(BF16)
    pick_ref[...] = pick
    get[1].wait()
    mine_ref[...] = dot(pick, tok_ref[...]).astype(BF16)
    get[2].wait()
    get[3].wait()


def select_kernel(capacity, pick_ref, mine_ref, sib_ref, *outs):
    core = lax.axis_index("tp") & 1
    depth = sib_ref.shape[1]
    here = pl.ds(pl.multiple_of(core * depth, depth), depth)
    there = pl.ds(pl.multiple_of((1 - core) * depth, depth), depth)
    other = dot(pick_ref[...], sib_ref[...]).astype(BF16)
    for k, out in enumerate(outs):
        rows = slice(k * capacity, (k + 1) * capacity)
        out[:, here] = mine_ref[rows, :]
        out[:, there] = other[rows]


def both(a_ref, b_ref):
    return jnp.concatenate([a_ref[...], b_ref[...]], axis=0)


def near_kernel(own_ref, sib_ref, w_ref, g_ref, u_ref):
    x = both(own_ref, sib_ref)
    g_ref[...] = dot(x, w_ref[0])
    u_ref[...] = dot(x, w_ref[1])


def first_near_kernel(own_ref, sib_ref, w_ref, gate_hbm, up_hbm, g_ref, u_ref, far_w_ref, sems):
    get = weight_copies(gate_hbm, up_hbm, far_w_ref, sems, 1)
    for g in get:
        g.start()
    near_kernel(own_ref, sib_ref, w_ref, g_ref, u_ref)
    for g in get:
        g.wait()


def far_kernel(capacity, far_ref, diag_ref, w_ref, g_ref, u_ref, h_ref):
    x = both(far_ref, diag_ref)
    gate = g_ref[...] + dot(x, w_ref[0])
    up = u_ref[...] + dot(x, w_ref[1])
    h = (gate / (1.0 + jnp.exp(-gate)) * up).astype(BF16)
    core = lax.axis_index("tp") & 1
    for i in range(4):
        k = i % 2
        block = 2 * k + (core ^ k ^ (i // 2))
        h_ref[pl.ds(pl.multiple_of(block * capacity, capacity), capacity), :] = h[i * capacity : (i + 1) * capacity]


def write_block(flip, h, factor, index, hess_hbm, buf, sems):
    wide = h.shape[1]
    part = wide // 4
    at = pl.ds(pl.multiple_of(index * wide, wide), wide)
    copies = []
    for i in range(4):
        rows = pl.ds(i * part, part)
        buf[rows, :] = dot(flip[rows, :], h) * factor
        copies.append(pltpu.make_async_copy(buf.at[rows, :], hess_hbm.at[0, rows, at], sems.at[i]))
        copies[-1].start()
    return copies


def hess_near_kernel(factor, capacity, ha, hb, sa, sb, flip_ref, hid_hbm, hess_hbm, buf, sems, out_sems):
    t = lax.axis_index("tp")
    e = lax.axis_index("ep")
    copies = []
    for o in range(8):
        src = (ha, hb)[o // 4].at[pl.ds((o % 4) * capacity, capacity), :]
        at = pl.ds(pl.multiple_of((e ^ o) * capacity, capacity), capacity)
        copies.append(pltpu.make_async_copy(src, hid_hbm.at[0, at, :], out_sems.at[o]))
        copies[-1].start()
    h = both(ha, hb)
    flip_ref[...] = h.astype(F32).T.astype(BF16)
    copies += write_block(flip_ref, h, factor, t, hess_hbm, buf.at[0], sems.at[0])
    copies += write_block(flip_ref, both(sa, sb), factor, t ^ 1, hess_hbm, buf.at[1], sems.at[1])
    for c in copies:
        c.wait()


def hess_far_kernel(factor, which, flip_ref, ha, hb, hess_in, hess_hbm, buf, sems):
    t = lax.axis_index("tp")
    for c in write_block(flip_ref, both(ha, hb), factor, t ^ which, hess_hbm, buf, sems):
        c.wait()


def call(kernel, out_shape, in_specs, out_specs, scratch=(), name=None, aliases={}, flops=0, moved=0, limit=LIMIT):
    return pl.pallas_call(
        kernel,
        out_shape=out_shape,
        in_specs=in_specs,
        out_specs=out_specs,
        scratch_shapes=list(scratch),
        input_output_aliases=aliases,
        name=name,
        cost_estimate=pl.CostEstimate(flops=flops, bytes_accessed=moved, transcendentals=0),
        compiler_params=pltpu.CompilerParams(vmem_limit_bytes=limit),
    )


def tie(x, after):
    return lax.optimization_barrier((x, after))[0]


def paired(tokens, expert_ids, gate_weight, up_weight):
    groups = 8
    tok_rows, depth = tokens.shape
    capacity = 2 * tok_rows * TOP // EXPERTS
    slots = groups * capacity
    wide = gate_weight.shape[2]
    full = wide * 4
    S = jax.ShapeDtypeStruct
    D = pltpu.SemaphoreType.DMA
    V = pltpu.VMEM

    def chips(x):
        return lax.ppermute(x, "tp", [(i, i ^ 2) for i in range(4)])

    def cores(x):
        return lax.ppermute(x, "tp", [(i, i ^ 1) for i in range(4)])

    def spread(k, x):
        pairs = [(e * 4 + t, (e ^ (2 * k + ((t ^ k) & 1))) * 4 + t) for e in range(8) for t in range(4)]
        return lax.ppermute(x, ("ep", "tp"), pairs)

    sib_tokens = cores(tokens)
    half = slots // 2
    weights = 4 * 2 * depth * 2 * wide
    ids, toks, gate_w, up_w = (
        pltpu.with_memory_space_constraint(a, pltpu.HBM) for a in (expert_ids.T, tokens, gate_weight, up_weight)
    )
    half_w = V((2, 2 * depth, wide), BF16)
    pick, mine, near_w = call(
        functools.partial(prepare_kernel, capacity),
        (S((half, tok_rows), BF16), S((half, depth), BF16), half_w),
        [HBM] * 4, (VMEM, VMEM, VMEM),
        (V(ids.shape, jnp.int32), V(tokens.shape, BF16), D((4,))), name="prepare",
        flops=2 * half * tok_rows * depth, moved=weights // 2,
    )(ids, toks, gate_w, up_w)
    out = call(
        functools.partial(select_kernel, capacity),
        (S((capacity, 2 * depth), BF16),) * 4, [VMEM] * 3, (VMEM,) * 4, name="select",
        flops=2 * half * tok_rows * depth,
    )(pick, mine, sib_tokens)
    got = [spread(k, out[k]) for k in range(4)]
    part = S((half, wide), F32)
    work = 4 * half * depth * 2 * wide

    def near(own, sib):
        return call(
            near_kernel, (part, part), [VMEM] * 3, (VMEM,) * 2, name="near", flops=work, moved=weights // 2,
        )(own, sib, near_w)

    def finish(far, diag, gate, up):
        return call(
            functools.partial(far_kernel, capacity), S((half, wide), BF16), [VMEM] * 5, VMEM, name="far",
            flops=work, moved=weights // 2,
        )(far, diag, far_w, gate, up)

    own1 = jnp.concatenate(got[:2])
    own2 = jnp.concatenate(got[2:])
    far1 = chips(own1)
    far2 = chips(own2)
    sib1 = cores(own1)
    sib2 = cores(own2)
    diag1 = cores(far1)
    gate1, up1, far_w = call(
        first_near_kernel, (part, part, half_w), [VMEM] * 3 + [HBM] * 2, (VMEM,) * 3, (D((4,)),), name="first_near",
        flops=work, moved=weights // 2,
    )(own1, tie(sib1, far1), near_w, gate_w, up_w)
    ha = finish(far1, diag1, gate1, up1)
    far_a = chips(ha)
    sib_a = cores(ha)
    far2 = tie(far2, ha)
    diag2 = cores(far2)
    gate2, up2 = near(own2, tie(sib2, far2))
    hb = finish(far2, diag2, gate2, up2)
    far_b = chips(hb)
    sib_b = cores(hb)
    diag_a = cores(far_a)

    factor = 2.0 / slots
    hess_shape = S((1, wide, full), F32)
    block = wide * wide * 4
    flip, hidden, hess = call(
        functools.partial(hess_near_kernel, factor, capacity),
        (S((wide, slots), BF16), S((1, slots, wide), BF16), hess_shape),
        [VMEM] * 4, (VMEM, ANY, ANY), (V((2, wide, wide), F32), D((2, 4)), D((8,))), name="hess_near",
        flops=4 * slots * wide * wide, moved=2 * block,
    )(ha, hb, sib_a, sib_b)

    def other(which, a, b, hess):
        return call(
            functools.partial(hess_far_kernel, factor, which), hess_shape,
            [VMEM, VMEM, VMEM, ANY], ANY, (V((wide, wide), F32), D((4,))), name="hess_%d" % which, aliases={3: 0},
            flops=2 * slots * wide * wide, moved=block,
        )(flip, a, b, hess)

    far_b = tie(far_b, flip)
    diag_b = cores(far_b)
    hess = other(2, far_a, far_b, hess)
    hess = other(3, diag_a, diag_b, hess)
    return hidden, hess


def general(tokens, expert_ids, gate_weight, up_weight):
    groups = lax.axis_size("ep")
    capacity = 2 * tokens.shape[0] * TOP // EXPERTS
    slots = groups * capacity
    member = jnp.any(expert_ids[:, :, None] == jnp.arange(groups, dtype=jnp.int32), axis=1).astype(jnp.int32)
    rank = jnp.cumsum(member, axis=0) - 1
    chosen = (member.T[:, None, :] > 0) & (rank.T[:, None, :] == jnp.arange(capacity, dtype=jnp.int32)[None, :, None])
    outgoing = jnp.einsum("gcj,jf->gcf", chosen.astype(BF16), tokens, preferred_element_type=F32).astype(BF16)
    arrived = lax.all_to_all(outgoing, "ep", split_axis=0, concat_axis=0, tiled=True)
    routed = lax.all_gather(arrived.reshape(slots, arrived.shape[2]), "tp", axis=1, tiled=True)
    gate = dot(routed, gate_weight[0])
    hidden = (jax.nn.silu(gate) * dot(routed, up_weight[0])).astype(BF16)
    whole = lax.all_gather(hidden, "tp", axis=1, tiled=True)
    hess = lax.dot_general(hidden, whole, (((0,), (0,)), ((), ())), preferred_element_type=F32) * (2.0 / slots)
    return hidden[None], hess[None]


def solution(mesh):
    body = paired if (mesh.shape["ep"], mesh.shape["tp"]) == (8, 4) else general
    return jax.shard_map(
        body,
        mesh=mesh,
        in_specs=(P("ep", "tp"), P("ep", None), P("ep", None, "tp"), P("ep", None, "tp")),
        out_specs=(P("ep", None, "tp"), P("ep", "tp", None)),
        check_vma=False,
    )
```

```python
import functools

import jax
import jax.numpy as jnp
from jax import lax
from jax.experimental import pallas as pl
from jax.experimental.pallas import tpu as pltpu
from jax.sharding import PartitionSpec as P

EXPERTS = 256
TOP = 8
BF16 = jnp.bfloat16
F32 = jnp.float32
VMEM = pl.BlockSpec(memory_space=pltpu.VMEM)
ANY = pl.BlockSpec(memory_space=pl.ANY)
HBM = pl.BlockSpec(memory_space=pltpu.HBM)
LIMIT = 40 * 1024 * 1024


DISTANCE = ((6, 2, 4), (7, 3, 5))
PARTS = ((0,), (1, 2), (3,))
ORDER = sum(PARTS, ())


def distance(core, k):
    return jnp.where(core == 0, DISTANCE[0][k], DISTANCE[1][k])


def dot(a, b):
    return lax.dot_general(a, b, (((1,), (0,)), ((), ())), preferred_element_type=F32)


def weight_copies(gate_hbm, up_hbm, w_ref, sems, chip):
    depth = w_ref.shape[1]
    at = pl.ds(pl.multiple_of(((lax.axis_index("tp") >> 1) ^ chip) * depth, depth), depth)
    return [pltpu.make_async_copy(w.at[0, at, :], w_ref.at[i], sems.at[i]) for i, w in enumerate((gate_hbm, up_hbm))]


def prepare_kernel(capacity, ids_hbm, tok_hbm, pick_ref, mine_ref, stay_ref, side_ref, ids_ref, tok_ref, sems):
    get = [
        pltpu.make_async_copy(ids_hbm, ids_ref, sems.at[0]),
        pltpu.make_async_copy(tok_hbm, tok_ref, sems.at[1]),
    ]
    for g in get:
        g.start()
    rows = ids_ref.shape[1]
    before = lax.broadcasted_iota(jnp.int32, (rows, rows), 0)
    after = lax.broadcasted_iota(jnp.int32, (rows, rows), 1)
    upto = jnp.where(before <= after, 1.0, 0.0).astype(BF16)
    want = lax.broadcasted_iota(jnp.int32, (5, capacity, rows), 1).astype(F32)
    core = lax.axis_index("tp") & 1
    step = lax.broadcasted_iota(jnp.int32, (8, rows), 0)
    offset = sum(jnp.where(step == k + 2, distance(core, k), 0) for k in range(3)) + jnp.where(step == 1, 1, 0)
    expert = lax.axis_index("ep") ^ offset
    get[0].wait()
    ids = ids_ref[...]
    hit = ids[0:1, :] == expert
    for k in range(1, ids.shape[0]):
        hit = hit | (ids[k : k + 1, :] == expert)
    count = dot(jnp.where(hit, 1.0, 0.0).astype(BF16), upto)
    slot = jnp.where(hit, count - 1.0, -1.0)[:5]
    pick = jnp.where(slot[:, None, :] == want, 1.0, 0.0)
    pick = pick.reshape(5 * capacity, rows).astype(BF16)
    pick_ref[...] = pick[2 * capacity :]
    get[1].wait()
    taken = dot(pick, tok_ref[...]).astype(BF16)
    stay_ref[...] = taken[:capacity]
    side_ref[...] = taken[capacity : 2 * capacity]
    mine_ref[...] = taken[2 * capacity :]


def select_kernel(capacity, pick_ref, mine_ref, sib_ref, *outs):
    core = lax.axis_index("tp") & 1
    depth = sib_ref.shape[1]
    here = pl.ds(pl.multiple_of(core * depth, depth), depth)
    there = pl.ds(pl.multiple_of((1 - core) * depth, depth), depth)
    other = dot(pick_ref[...], sib_ref[...]).astype(BF16)
    for k, out in enumerate(outs):
        rows = slice(k * capacity, (k + 1) * capacity)
        out[:, here] = mine_ref[rows, :]
        out[:, there] = other[rows]


def load_kernel(after_ref, gate_hbm, up_hbm, near_ref, far_ref, near_sems, far_sems):
    get = weight_copies(gate_hbm, up_hbm, near_ref, near_sems, 0) + weight_copies(gate_hbm, up_hbm, far_ref, far_sems, 1)
    for g in get:
        g.start()
    for g in get:
        g.wait()


def assemble(capacity, one_ref, other_ref, x_ref):
    core = lax.axis_index("tp") & 1
    depth = x_ref.shape[1] // 2
    for c, ref in ((core, one_ref), (1 - core, other_ref)):
        lanes = pl.ds(pl.multiple_of(c * depth, depth), depth)
        for at, k in enumerate(ORDER):
            block = ref[pl.ds(at * capacity, capacity), :]
            if k == 0:
                x_ref[pl.ds(0, capacity), lanes] = block[:, :depth]
                x_ref[pl.ds(capacity, capacity), lanes] = block[:, depth:]
            else:
                x_ref[pl.ds(pl.multiple_of(distance(c, k - 1) * capacity, capacity), capacity), :] = block


def near_kernel(capacity, own_ref, sib_ref, w_ref, g_ref, u_ref, x_ref):
    assemble(capacity, own_ref, sib_ref, x_ref)
    g_ref[...] = dot(x_ref[...], w_ref[0])
    u_ref[...] = dot(x_ref[...], w_ref[1])


def far_kernel(capacity, far_ref, diag_ref, w_ref, g_ref, u_ref, h_ref, x_ref):
    assemble(capacity, far_ref, diag_ref, x_ref)
    gate = g_ref[...] + dot(x_ref[...], w_ref[0])
    up = u_ref[...] + dot(x_ref[...], w_ref[1])
    h_ref[...] = (gate / (1.0 + jnp.exp(-gate)) * up).astype(BF16)


def write_block(flip, h, factor, index, hess_hbm, buf, sems):
    wide = h.shape[1]
    part = wide // 4
    at = pl.ds(pl.multiple_of(index * wide, wide), wide)
    copies = []
    for i in range(4):
        rows = pl.ds(i * part, part)
        buf[rows, :] = dot(flip[rows, :], h) * factor
        copies.append(pltpu.make_async_copy(buf.at[rows, :], hess_hbm.at[0, rows, at], sems.at[i]))
        copies[-1].start()
    return copies


def hess_near_kernel(factor, capacity, h_ref, sib_ref, flip_ref, hid_hbm, hess_hbm, buf, sems, out_sems):
    t = lax.axis_index("tp")
    e = lax.axis_index("ep")
    copies = []
    for o in range(8):
        src = h_ref.at[pl.ds(o * capacity, capacity), :]
        at = pl.ds(pl.multiple_of((e ^ o) * capacity, capacity), capacity)
        copies.append(pltpu.make_async_copy(src, hid_hbm.at[0, at, :], out_sems.at[o]))
        copies[-1].start()
    flip_ref[...] = h_ref[...].astype(F32).T.astype(BF16)
    copies += write_block(flip_ref, h_ref[...], factor, t, hess_hbm, buf.at[0], sems.at[0])
    copies += write_block(flip_ref, sib_ref[...], factor, t ^ 1, hess_hbm, buf.at[1], sems.at[1])
    for c in copies:
        c.wait()


def hess_far_kernel(factor, which, flip_ref, h_ref, hess_in, hess_hbm, buf, sems):
    t = lax.axis_index("tp")
    for c in write_block(flip_ref, h_ref[...], factor, t ^ which, hess_hbm, buf, sems):
        c.wait()


def call(kernel, out_shape, in_specs, out_specs, scratch=(), name=None, aliases={}, flops=0, moved=0, limit=LIMIT):
    return pl.pallas_call(
        kernel,
        out_shape=out_shape,
        in_specs=in_specs,
        out_specs=out_specs,
        scratch_shapes=list(scratch),
        input_output_aliases=aliases,
        name=name,
        cost_estimate=pl.CostEstimate(flops=flops, bytes_accessed=moved, transcendentals=0),
        compiler_params=pltpu.CompilerParams(vmem_limit_bytes=limit),
    )


def tie(x, after):
    return lax.optimization_barrier((x, after))[0]


def paired(tokens, expert_ids, gate_weight, up_weight):
    groups = 8
    tok_rows, depth = tokens.shape
    capacity = 2 * tok_rows * TOP // EXPERTS
    slots = groups * capacity
    wide = gate_weight.shape[2]
    full = wide * 4
    S = jax.ShapeDtypeStruct
    D = pltpu.SemaphoreType.DMA
    V = pltpu.VMEM

    def chips(x):
        return lax.ppermute(x, "tp", [(i, i ^ 2) for i in range(4)])

    def cores(x):
        return lax.ppermute(x, "tp", [(i, i ^ 1) for i in range(4)])

    def spread(k, x):
        pairs = [(e * 4 + t, (e ^ DISTANCE[t & 1][k]) * 4 + t) for e in range(8) for t in range(4)]
        return lax.ppermute(x, ("ep", "tp"), pairs)

    sib_tokens = cores(tokens)
    weights = 4 * 2 * depth * 2 * wide
    ids, toks, gate_w, up_w = (
        pltpu.with_memory_space_constraint(a, pltpu.HBM) for a in (expert_ids.T, tokens, gate_weight, up_weight)
    )
    single = S((capacity, depth), BF16)
    pick, mine, stay, side = call(
        functools.partial(prepare_kernel, capacity),
        (S((3 * capacity, tok_rows), BF16), S((3 * capacity, depth), BF16), single, single),
        [HBM] * 2, (VMEM,) * 4,
        (V(ids.shape, jnp.int32), V(tokens.shape, BF16), D((2,))), name="prepare",
        flops=10 * capacity * tok_rows * depth, moved=tokens.size * 2,
    )(ids, toks)
    side = lax.ppermute(side, "ep", [(e, e ^ 1) for e in range(8)])
    out = call(
        functools.partial(select_kernel, capacity),
        (S((capacity, 2 * depth), BF16),) * 3, [VMEM] * 3, (VMEM,) * 3, name="select",
        flops=6 * capacity * tok_rows * depth,
    )(pick, mine, sib_tokens)
    got = [jnp.concatenate([stay, side], axis=1)] + [spread(k, out[k]) for k in range(3)]
    half_w = V((2, 2 * depth, wide), BF16)
    part = S((slots, wide), F32)
    work = 4 * slots * depth * 2 * wide
    parts = [jnp.concatenate([got[k] for k in part]) for part in PARTS]
    far = jnp.concatenate([chips(part) for part in parts])
    own = jnp.concatenate(parts)
    sib = cores(own)
    near_w, far_w = call(
        load_kernel, (half_w, half_w), [VMEM] + [HBM] * 2, (VMEM,) * 2, (D((2,)), D((2,))), name="load", moved=weights,
    )(own, gate_w, up_w)
    far = tie(far, far_w)
    diag = cores(far)
    x = V((slots, 2 * depth), BF16)
    gate, up = call(
        functools.partial(near_kernel, capacity), (part, part), [VMEM] * 3, (VMEM,) * 2, (x,), name="near",
        flops=work, moved=weights // 2,
    )(own, tie(sib, far), near_w)
    hidden = call(
        functools.partial(far_kernel, capacity), S((slots, wide), BF16), [VMEM] * 5, VMEM, (x,), name="far",
        flops=work, moved=weights // 2,
    )(far, diag, far_w, gate, up)

    factor = 2.0 / slots
    hess_shape = S((1, wide, full), F32)
    block = wide * wide * 4
    far_h = chips(hidden)
    sib_h = cores(hidden)
    flip, hidden, hess = call(
        functools.partial(hess_near_kernel, factor, capacity),
        (S((wide, slots), BF16), S((1, slots, wide), BF16), hess_shape),
        [VMEM] * 2, (VMEM, ANY, ANY), (V((2, wide, wide), F32), D((2, 4)), D((8,))), name="hess_near",
        flops=4 * slots * wide * wide, moved=2 * block,
    )(hidden, sib_h)

    def other(which, h, hess):
        return call(
            functools.partial(hess_far_kernel, factor, which), hess_shape,
            [VMEM, VMEM, ANY], ANY, (V((wide, wide), F32), D((4,))), name="hess_%d" % which, aliases={2: 0},
            flops=2 * slots * wide * wide, moved=block,
        )(flip, h, hess)

    far_h = tie(far_h, flip)
    diag_h = cores(far_h)
    hess = other(2, far_h, hess)
    hess = other(3, diag_h, hess)
    return hidden, hess


def general(tokens, expert_ids, gate_weight, up_weight):
    groups = lax.axis_size("ep")
    capacity = 2 * tokens.shape[0] * TOP // EXPERTS
    slots = groups * capacity
    member = jnp.any(expert_ids[:, :, None] == jnp.arange(groups, dtype=jnp.int32), axis=1).astype(jnp.int32)
    rank = jnp.cumsum(member, axis=0) - 1
    chosen = (member.T[:, None, :] > 0) & (rank.T[:, None, :] == jnp.arange(capacity, dtype=jnp.int32)[None, :, None])
    outgoing = jnp.einsum("gcj,jf->gcf", chosen.astype(BF16), tokens, preferred_element_type=F32).astype(BF16)
    arrived = lax.all_to_all(outgoing, "ep", split_axis=0, concat_axis=0, tiled=True)
    routed = lax.all_gather(arrived.reshape(slots, arrived.shape[2]), "tp", axis=1, tiled=True)
    gate = dot(routed, gate_weight[0])
    hidden = (jax.nn.silu(gate) * dot(routed, up_weight[0])).astype(BF16)
    whole = lax.all_gather(hidden, "tp", axis=1, tiled=True)
    hess = lax.dot_general(hidden, whole, (((0,), (0,)), ((), ())), preferred_element_type=F32) * (2.0 / slots)
    return hidden[None], hess[None]


def solution(mesh):
    body = paired if (mesh.shape["ep"], mesh.shape["tp"]) == (8, 4) else general
    return jax.shard_map(
        body,
        mesh=mesh,
        in_specs=(P("ep", "tp"), P("ep", None), P("ep", None, "tp"), P("ep", None, "tp")),
        out_specs=(P("ep", None, "tp"), P("ep", "tp", None)),
        check_vma=False,
    )
```

```python
import functools

import jax
import jax.numpy as jnp
from jax import lax
from jax.experimental import pallas as pl
from jax.experimental.pallas import tpu as pltpu
from jax.sharding import PartitionSpec as P

EXPERTS = 256
TOP = 8
BF16 = jnp.bfloat16
F32 = jnp.float32
VMEM = pl.BlockSpec(memory_space=pltpu.VMEM)
ANY = pl.BlockSpec(memory_space=pl.ANY)
HBM = pl.BlockSpec(memory_space=pltpu.HBM)
LIMIT = 40 * 1024 * 1024


DISTANCE = ((6, 2, 4), (7, 3, 5))
PARTS = ((1, 2), (3,), (0,))
ORDER = sum(PARTS, ())


def distance(core, k):
    return jnp.where(core == 0, DISTANCE[0][k], DISTANCE[1][k])


def dot(a, b):
    return lax.dot_general(a, b, (((1,), (0,)), ((), ())), preferred_element_type=F32)


def weight_copies(gate_hbm, up_hbm, w_ref, sems, chip):
    depth = w_ref.shape[1]
    at = pl.ds(pl.multiple_of(((lax.axis_index("tp") >> 1) ^ chip) * depth, depth), depth)
    return [pltpu.make_async_copy(w.at[0, at, :], w_ref.at[i], sems.at[i]) for i, w in enumerate((gate_hbm, up_hbm))]


def prepare_kernel(capacity, ids_hbm, tok_hbm, pick_ref, mine_ref, stay_ref, side_ref, ids_ref, tok_ref, sems):
    get = [
        pltpu.make_async_copy(ids_hbm, ids_ref, sems.at[0]),
        pltpu.make_async_copy(tok_hbm, tok_ref, sems.at[1]),
    ]
    for g in get:
        g.start()
    rows = ids_ref.shape[1]
    before = lax.broadcasted_iota(jnp.int32, (rows, rows), 0)
    after = lax.broadcasted_iota(jnp.int32, (rows, rows), 1)
    upto = jnp.where(before <= after, 1.0, 0.0).astype(BF16)
    want = lax.broadcasted_iota(jnp.int32, (5, capacity, rows), 1).astype(F32)
    core = lax.axis_index("tp") & 1
    step = lax.broadcasted_iota(jnp.int32, (8, rows), 0)
    offset = sum(jnp.where(step == k + 2, distance(core, k), 0) for k in range(3)) + jnp.where(step == 1, 1, 0)
    expert = lax.axis_index("ep") ^ offset
    get[0].wait()
    ids = ids_ref[...]
    hit = ids[0:1, :] == expert
    for k in range(1, ids.shape[0]):
        hit = hit | (ids[k : k + 1, :] == expert)
    count = dot(jnp.where(hit, 1.0, 0.0).astype(BF16), upto)
    slot = jnp.where(hit, count - 1.0, -1.0)[:5]
    pick = jnp.where(slot[:, None, :] == want, 1.0, 0.0)
    pick = pick.reshape(5 * capacity, rows).astype(BF16)
    pick_ref[...] = pick[2 * capacity :]
    get[1].wait()
    taken = dot(pick, tok_ref[...]).astype(BF16)
    stay_ref[...] = taken[:capacity]
    side_ref[...] = taken[capacity : 2 * capacity]
    mine_ref[...] = taken[2 * capacity :]


def select_kernel(capacity, pick_ref, mine_ref, sib_ref, *outs):
    core = lax.axis_index("tp") & 1
    depth = sib_ref.shape[1]
    here = pl.ds(pl.multiple_of(core * depth, depth), depth)
    there = pl.ds(pl.multiple_of((1 - core) * depth, depth), depth)
    other = dot(pick_ref[...], sib_ref[...]).astype(BF16)
    for k, out in enumerate(outs):
        rows = slice(k * capacity, (k + 1) * capacity)
        out[:, here] = mine_ref[rows, :]
        out[:, there] = other[rows]


def load_kernel(after_ref, gate_hbm, up_hbm, near_ref, far_ref, near_sems, far_sems):
    get = weight_copies(gate_hbm, up_hbm, near_ref, near_sems, 0) + weight_copies(gate_hbm, up_hbm, far_ref, far_sems, 1)
    for g in get:
        g.start()
    for g in get:
        g.wait()


def assemble(capacity, one_ref, other_ref, x_ref):
    core = lax.axis_index("tp") & 1
    depth = x_ref.shape[1] // 2
    for c, ref in ((core, one_ref), (1 - core, other_ref)):
        lanes = pl.ds(pl.multiple_of(c * depth, depth), depth)
        for at, k in enumerate(ORDER):
            block = ref[pl.ds(at * capacity, capacity), :]
            if k == 0:
                x_ref[pl.ds(0, capacity), lanes] = block[:, :depth]
                x_ref[pl.ds(capacity, capacity), lanes] = block[:, depth:]
            else:
                x_ref[pl.ds(pl.multiple_of(distance(c, k - 1) * capacity, capacity), capacity), :] = block


def near_kernel(capacity, own_ref, sib_ref, w_ref, g_ref, u_ref, x_ref):
    assemble(capacity, own_ref, sib_ref, x_ref)
    g_ref[...] = dot(x_ref[...], w_ref[0])
    u_ref[...] = dot(x_ref[...], w_ref[1])


def far_kernel(capacity, far_ref, diag_ref, w_ref, g_ref, u_ref, h_ref, x_ref):
    assemble(capacity, far_ref, diag_ref, x_ref)
    gate = g_ref[...] + dot(x_ref[...], w_ref[0])
    up = u_ref[...] + dot(x_ref[...], w_ref[1])
    h_ref[...] = (gate / (1.0 + jnp.exp(-gate)) * up).astype(BF16)


def write_block(flip, h, factor, index, hess_hbm, buf, sems):
    wide = h.shape[1]
    part = wide // 4
    at = pl.ds(pl.multiple_of(index * wide, wide), wide)
    copies = []
    for i in range(4):
        rows = pl.ds(i * part, part)
        buf[rows, :] = dot(flip[rows, :], h) * factor
        copies.append(pltpu.make_async_copy(buf.at[rows, :], hess_hbm.at[0, rows, at], sems.at[i]))
        copies[-1].start()
    return copies


def hess_near_kernel(factor, capacity, h_ref, sib_ref, flip_ref, hid_hbm, hess_hbm, buf, sems, out_sems):
    t = lax.axis_index("tp")
    e = lax.axis_index("ep")
    copies = []
    for o in range(8):
        src = h_ref.at[pl.ds(o * capacity, capacity), :]
        at = pl.ds(pl.multiple_of((e ^ o) * capacity, capacity), capacity)
        copies.append(pltpu.make_async_copy(src, hid_hbm.at[0, at, :], out_sems.at[o]))
        copies[-1].start()
    slots = h_ref.shape[0]
    flip_ref[...] = h_ref[...].astype(F32).T.astype(BF16)
    copies += write_block(flip_ref, h_ref[...], factor, t, hess_hbm, buf.at[0], sems.at[0])
    copies += write_block(flip_ref, sib_ref[pl.ds(pl.multiple_of((1 - (t & 1)) * slots, slots), slots), :], factor, t ^ 1, hess_hbm, buf.at[1], sems.at[1])
    for c in copies:
        c.wait()


def hess_far_kernel(factor, which, flip_ref, h_ref, hess_in, hess_hbm, buf, sems):
    t = lax.axis_index("tp")
    for c in write_block(flip_ref, h_ref[...], factor, t ^ which, hess_hbm, buf, sems):
        c.wait()


def call(kernel, out_shape, in_specs, out_specs, scratch=(), name=None, aliases={}, flops=0, moved=0, limit=LIMIT):
    return pl.pallas_call(
        kernel,
        out_shape=out_shape,
        in_specs=in_specs,
        out_specs=out_specs,
        scratch_shapes=list(scratch),
        input_output_aliases=aliases,
        name=name,
        cost_estimate=pl.CostEstimate(flops=flops, bytes_accessed=moved, transcendentals=0),
        compiler_params=pltpu.CompilerParams(vmem_limit_bytes=limit),
    )


def tie(x, after):
    return lax.optimization_barrier((x, after))[0]


def paired(tokens, expert_ids, gate_weight, up_weight):
    groups = 8
    tok_rows, depth = tokens.shape
    capacity = 2 * tok_rows * TOP // EXPERTS
    slots = groups * capacity
    wide = gate_weight.shape[2]
    full = wide * 4
    S = jax.ShapeDtypeStruct
    D = pltpu.SemaphoreType.DMA
    V = pltpu.VMEM

    def chips(x):
        return lax.ppermute(x, "tp", [(i, i ^ 2) for i in range(4)])

    def cores(x):
        return lax.ppermute(x, "tp", [(i, i ^ 1) for i in range(4)])

    def spread(k, x):
        pairs = [(e * 4 + t, (e ^ DISTANCE[t & 1][k]) * 4 + t) for e in range(8) for t in range(4)]
        return lax.ppermute(x, ("ep", "tp"), pairs)

    sib_tokens = cores(tokens)
    weights = 4 * 2 * depth * 2 * wide
    ids, toks, gate_w, up_w = (
        pltpu.with_memory_space_constraint(a, pltpu.HBM) for a in (expert_ids.T, tokens, gate_weight, up_weight)
    )
    single = S((capacity, depth), BF16)
    pick, mine, stay, side = call(
        functools.partial(prepare_kernel, capacity),
        (S((3 * capacity, tok_rows), BF16), S((3 * capacity, depth), BF16), single, single),
        [HBM] * 2, (VMEM,) * 4,
        (V(ids.shape, jnp.int32), V(tokens.shape, BF16), D((2,))), name="prepare",
        flops=10 * capacity * tok_rows * depth, moved=tokens.size * 2,
    )(ids, toks)
    side = lax.ppermute(side, "ep", [(e, e ^ 1) for e in range(8)])
    out = call(
        functools.partial(select_kernel, capacity),
        (S((capacity, 2 * depth), BF16),) * 3, [VMEM] * 3, (VMEM,) * 3, name="select",
        flops=6 * capacity * tok_rows * depth,
    )(pick, mine, sib_tokens)
    got = [jnp.concatenate([stay, side], axis=1)] + [spread(k, out[k]) for k in range(3)]
    half_w = V((2, 2 * depth, wide), BF16)
    part = S((slots, wide), F32)
    work = 4 * slots * depth * 2 * wide
    parts = [jnp.concatenate([got[k] for k in part]) for part in PARTS]
    far = jnp.concatenate([chips(part) for part in parts])
    own = jnp.concatenate(parts)
    sib = cores(own)
    near_w, far_w = call(
        load_kernel, (half_w, half_w), [VMEM] + [HBM] * 2, (VMEM,) * 2, (D((2,)), D((2,))), name="load", moved=weights,
    )(own, gate_w, up_w)
    early = 2 * capacity
    late = tie(far[early:], (far_w, far[:early]))
    diag = jnp.concatenate([cores(far[:early]), cores(late)])
    far = jnp.concatenate([far[:early], late])
    x = V((slots, 2 * depth), BF16)
    gate, up = call(
        functools.partial(near_kernel, capacity), (part, part), [VMEM] * 3, (VMEM,) * 2, (x,), name="near",
        flops=work, moved=weights // 2,
    )(own, tie(sib, far), near_w)
    hidden = call(
        functools.partial(far_kernel, capacity), S((slots, wide), BF16), [VMEM] * 5, VMEM, (x,), name="far",
        flops=work, moved=weights // 2,
    )(far, diag, far_w, gate, up)

    factor = 2.0 / slots
    hess_shape = S((1, wide, full), F32)
    block = wide * wide * 4
    far_h = chips(hidden)
    pair_h = lax.all_gather(hidden, "tp", axis=0, tiled=True, axis_index_groups=[[0, 1], [2, 3]])
    flip, hidden, hess = call(
        functools.partial(hess_near_kernel, factor, capacity),
        (S((wide, slots), BF16), S((1, slots, wide), BF16), hess_shape),
        [VMEM] * 2, (VMEM, ANY, ANY), (V((2, wide, wide), F32), D((2, 4)), D((8,))), name="hess_near",
        flops=4 * slots * wide * wide, moved=2 * block,
    )(hidden, pair_h)

    def other(which, h, hess):
        return call(
            functools.partial(hess_far_kernel, factor, which), hess_shape,
            [VMEM, VMEM, ANY], ANY, (V((wide, wide), F32), D((4,))), name="hess_%d" % which, aliases={2: 0},
            flops=2 * slots * wide * wide, moved=block,
        )(flip, h, hess)

    far_h = tie(far_h, flip)
    diag_h = cores(far_h)
    hess = other(2, far_h, hess)
    hess = other(3, diag_h, hess)
    return hidden, hess


def general(tokens, expert_ids, gate_weight, up_weight):
    groups = lax.axis_size("ep")
    capacity = 2 * tokens.shape[0] * TOP // EXPERTS
    slots = groups * capacity
    member = jnp.any(expert_ids[:, :, None] == jnp.arange(groups, dtype=jnp.int32), axis=1).astype(jnp.int32)
    rank = jnp.cumsum(member, axis=0) - 1
    chosen = (member.T[:, None, :] > 0) & (rank.T[:, None, :] == jnp.arange(capacity, dtype=jnp.int32)[None, :, None])
    outgoing = jnp.einsum("gcj,jf->gcf", chosen.astype(BF16), tokens, preferred_element_type=F32).astype(BF16)
    arrived = lax.all_to_all(outgoing, "ep", split_axis=0, concat_axis=0, tiled=True)
    routed = lax.all_gather(arrived.reshape(slots, arrived.shape[2]), "tp", axis=1, tiled=True)
    gate = dot(routed, gate_weight[0])
    hidden = (jax.nn.silu(gate) * dot(routed, up_weight[0])).astype(BF16)
    whole = lax.all_gather(hidden, "tp", axis=1, tiled=True)
    hess = lax.dot_general(hidden, whole, (((0,), (0,)), ((), ())), preferred_element_type=F32) * (2.0 / slots)
    return hidden[None], hess[None]


def solution(mesh):
    body = paired if (mesh.shape["ep"], mesh.shape["tp"]) == (8, 4) else general
    return jax.shard_map(
        body,
        mesh=mesh,
        in_specs=(P("ep", "tp"), P("ep", None), P("ep", None, "tp"), P("ep", None, "tp")),
        out_specs=(P("ep", None, "tp"), P("ep", "tp", None)),
        check_vma=False,
    )
```

```python
import functools

import jax
import jax.numpy as jnp
from jax import lax
from jax.experimental import pallas as pl
from jax.experimental.pallas import tpu as pltpu
from jax.sharding import PartitionSpec as P

EXPERTS = 256
TOP = 8
BF16 = jnp.bfloat16
F32 = jnp.float32
VMEM = pl.BlockSpec(memory_space=pltpu.VMEM)
ANY = pl.BlockSpec(memory_space=pl.ANY)
HBM = pl.BlockSpec(memory_space=pltpu.HBM)
LIMIT = 40 * 1024 * 1024


DISTANCE = ((4, 5, 2), (7, 6, 3))
PARTS = ((1, 2), (0,), (3,))
ORDER = sum(PARTS, ())


def distance(core, k):
    return jnp.where(core == 0, DISTANCE[0][k], DISTANCE[1][k])


def dot(a, b):
    return lax.dot_general(a, b, (((1,), (0,)), ((), ())), preferred_element_type=F32)


def weight_copies(gate_hbm, up_hbm, w_ref, sems, chip):
    depth = w_ref.shape[1]
    at = pl.ds(pl.multiple_of(((lax.axis_index("tp") >> 1) ^ chip) * depth, depth), depth)
    return [pltpu.make_async_copy(w.at[0, at, :], w_ref.at[i], sems.at[i]) for i, w in enumerate((gate_hbm, up_hbm))]


def prepare_kernel(capacity, ids_hbm, tok_hbm, pick_ref, mine_ref, stay_ref, side_ref, ids_ref, tok_ref, sems):
    get = [
        pltpu.make_async_copy(ids_hbm, ids_ref, sems.at[0]),
        pltpu.make_async_copy(tok_hbm, tok_ref, sems.at[1]),
    ]
    for g in get:
        g.start()
    rows = ids_ref.shape[1]
    before = lax.broadcasted_iota(jnp.int32, (rows, rows), 0)
    after = lax.broadcasted_iota(jnp.int32, (rows, rows), 1)
    upto = jnp.where(before <= after, 1.0, 0.0).astype(BF16)
    want = lax.broadcasted_iota(jnp.int32, (5, capacity, rows), 1).astype(F32)
    core = lax.axis_index("tp") & 1
    step = lax.broadcasted_iota(jnp.int32, (8, rows), 0)
    offset = sum(jnp.where(step == k + 2, distance(core, k), 0) for k in range(3)) + jnp.where(step == 1, 1, 0)
    expert = lax.axis_index("ep") ^ offset
    get[0].wait()
    ids = ids_ref[...]
    hit = ids[0:1, :] == expert
    for k in range(1, ids.shape[0]):
        hit = hit | (ids[k : k + 1, :] == expert)
    count = dot(jnp.where(hit, 1.0, 0.0).astype(BF16), upto)
    slot = jnp.where(hit, count - 1.0, -1.0)[:5]
    pick = jnp.where(slot[:, None, :] == want, 1.0, 0.0)
    pick = pick.reshape(5 * capacity, rows).astype(BF16)
    pick_ref[...] = pick[2 * capacity :]
    get[1].wait()
    taken = dot(pick, tok_ref[...]).astype(BF16)
    stay_ref[...] = taken[:capacity]
    side_ref[...] = taken[capacity : 2 * capacity]
    mine_ref[...] = taken[2 * capacity :]


def select_kernel(capacity, pick_ref, mine_ref, sib_ref, *outs):
    core = lax.axis_index("tp") & 1
    depth = sib_ref.shape[1]
    here = pl.ds(pl.multiple_of(core * depth, depth), depth)
    there = pl.ds(pl.multiple_of((1 - core) * depth, depth), depth)
    other = dot(pick_ref[...], sib_ref[...]).astype(BF16)
    for k, out in enumerate(outs):
        rows = slice(k * capacity, (k + 1) * capacity)
        out[:, here] = mine_ref[rows, :]
        out[:, there] = other[rows]


def load_kernel(after_ref, gate_hbm, up_hbm, near_ref, far_ref, near_sems, far_sems):
    get = weight_copies(gate_hbm, up_hbm, near_ref, near_sems, 0) + weight_copies(gate_hbm, up_hbm, far_ref, far_sems, 1)
    for g in get:
        g.start()
    for g in get:
        g.wait()


def assemble(capacity, one_ref, other_ref, x_ref):
    core = lax.axis_index("tp") & 1
    depth = x_ref.shape[1] // 2
    for c, ref in ((core, one_ref), (1 - core, other_ref)):
        lanes = pl.ds(pl.multiple_of(c * depth, depth), depth)
        for at, k in enumerate(ORDER):
            block = ref[pl.ds(at * capacity, capacity), :]
            if k == 0:
                x_ref[pl.ds(0, capacity), lanes] = block[:, :depth]
                x_ref[pl.ds(capacity, capacity), lanes] = block[:, depth:]
            else:
                x_ref[pl.ds(pl.multiple_of(distance(c, k - 1) * capacity, capacity), capacity), :] = block


def near_kernel(capacity, own_ref, sib_ref, w_ref, g_ref, u_ref, x_ref):
    assemble(capacity, own_ref, sib_ref, x_ref)
    g_ref[...] = dot(x_ref[...], w_ref[0])
    u_ref[...] = dot(x_ref[...], w_ref[1])


def far_kernel(capacity, far_ref, diag_ref, w_ref, g_ref, u_ref, h_ref, x_ref):
    assemble(capacity, far_ref, diag_ref, x_ref)
    gate = g_ref[...] + dot(x_ref[...], w_ref[0])
    up = u_ref[...] + dot(x_ref[...], w_ref[1])
    h_ref[...] = (gate / (1.0 + jnp.exp(-gate)) * up).astype(BF16)


def write_block(flip, h, factor, index, hess_hbm, buf, sems):
    wide = h.shape[1]
    part = wide // 4
    at = pl.ds(pl.multiple_of(index * wide, wide), wide)
    copies = []
    for i in range(4):
        rows = pl.ds(i * part, part)
        buf[rows, :] = dot(flip[rows, :], h) * factor
        copies.append(pltpu.make_async_copy(buf.at[rows, :], hess_hbm.at[0, rows, at], sems.at[i]))
        copies[-1].start()
    return copies


def hess_near_kernel(factor, capacity, h_ref, sib_ref, flip_ref, hid_hbm, hess_hbm, buf, sems, out_sems):
    t = lax.axis_index("tp")
    e = lax.axis_index("ep")
    copies = []
    for o in range(8):
        src = h_ref.at[pl.ds(o * capacity, capacity), :]
        at = pl.ds(pl.multiple_of((e ^ o) * capacity, capacity), capacity)
        copies.append(pltpu.make_async_copy(src, hid_hbm.at[0, at, :], out_sems.at[o]))
        copies[-1].start()
    slots = h_ref.shape[0]
    flip_ref[...] = h_ref[...].astype(F32).T.astype(BF16)
    copies += write_block(flip_ref, h_ref[...], factor, t, hess_hbm, buf.at[0], sems.at[0])
    copies += write_block(flip_ref, sib_ref[pl.ds(pl.multiple_of((1 - (t & 1)) * slots, slots), slots), :], factor, t ^ 1, hess_hbm, buf.at[1], sems.at[1])
    for c in copies:
        c.wait()


def hess_far_kernel(factor, which, flip_ref, h_ref, hess_in, hess_hbm, buf, sems):
    t = lax.axis_index("tp")
    for c in write_block(flip_ref, h_ref[...], factor, t ^ which, hess_hbm, buf, sems):
        c.wait()


def call(kernel, out_shape, in_specs, out_specs, scratch=(), name=None, aliases={}, flops=0, moved=0, limit=LIMIT):
    return pl.pallas_call(
        kernel,
        out_shape=out_shape,
        in_specs=in_specs,
        out_specs=out_specs,
        scratch_shapes=list(scratch),
        input_output_aliases=aliases,
        name=name,
        cost_estimate=pl.CostEstimate(flops=flops, bytes_accessed=moved, transcendentals=0),
        compiler_params=pltpu.CompilerParams(vmem_limit_bytes=limit),
    )


def tie(x, after):
    return lax.optimization_barrier((x, after))[0]


def paired(tokens, expert_ids, gate_weight, up_weight):
    groups = 8
    tok_rows, depth = tokens.shape
    capacity = 2 * tok_rows * TOP // EXPERTS
    slots = groups * capacity
    wide = gate_weight.shape[2]
    full = wide * 4
    S = jax.ShapeDtypeStruct
    D = pltpu.SemaphoreType.DMA
    V = pltpu.VMEM

    def chips(x):
        return lax.ppermute(x, "tp", [(i, i ^ 2) for i in range(4)])

    def cores(x):
        return lax.ppermute(x, "tp", [(i, i ^ 1) for i in range(4)])

    def spread(k, x, other_chip=0):
        pairs = [(e * 4 + t, (e ^ DISTANCE[t & 1][k]) * 4 + (t ^ other_chip)) for e in range(8) for t in range(4)]
        return lax.ppermute(x, ("ep", "tp"), pairs)

    sib_tokens = cores(tokens)
    weights = 4 * 2 * depth * 2 * wide
    ids, toks, gate_w, up_w = (
        pltpu.with_memory_space_constraint(a, pltpu.HBM) for a in (expert_ids.T, tokens, gate_weight, up_weight)
    )
    single = S((capacity, depth), BF16)
    pick, mine, stay, side = call(
        functools.partial(prepare_kernel, capacity),
        (S((3 * capacity, tok_rows), BF16), S((3 * capacity, depth), BF16), single, single),
        [HBM] * 2, (VMEM,) * 4,
        (V(ids.shape, jnp.int32), V(tokens.shape, BF16), D((2,))), name="prepare",
        flops=10 * capacity * tok_rows * depth, moved=tokens.size * 2,
    )(ids, toks)
    side = lax.ppermute(side, "ep", [(e, e ^ 1) for e in range(8)])
    out = call(
        functools.partial(select_kernel, capacity),
        (S((capacity, 2 * depth), BF16),) * 3, [VMEM] * 3, (VMEM,) * 3, name="select",
        flops=6 * capacity * tok_rows * depth,
    )(pick, mine, sib_tokens)
    got = [jnp.concatenate([stay, side], axis=1)] + [spread(k, out[k]) for k in range(3)]
    half_w = V((2, 2 * depth, wide), BF16)
    part = S((slots, wide), F32)
    work = 4 * slots * depth * 2 * wide
    parts = [jnp.concatenate([got[k] for k in part]) for part in PARTS]
    far = jnp.concatenate([chips(part) for part in parts[:-1]] + [spread(k - 1, out[k - 1], 2) for k in PARTS[-1]])
    own = jnp.concatenate(parts)
    sib = cores(own)
    near_w, far_w = call(
        load_kernel, (half_w, half_w), [VMEM] + [HBM] * 2, (VMEM,) * 2, (D((2,)), D((2,))), name="load", moved=weights,
    )(own, gate_w, up_w)
    early = 2 * capacity
    late = tie(far[early:], far_w)
    diag = jnp.concatenate([cores(far[:early]), cores(late)])
    far = jnp.concatenate([far[:early], late])
    x = V((slots, 2 * depth), BF16)
    gate, up = call(
        functools.partial(near_kernel, capacity), (part, part), [VMEM] * 3, (VMEM,) * 2, (x,), name="near",
        flops=work, moved=weights // 2,
    )(own, tie(sib, far), near_w)
    hidden = call(
        functools.partial(far_kernel, capacity), S((slots, wide), BF16), [VMEM] * 5, VMEM, (x,), name="far",
        flops=work, moved=weights // 2,
    )(far, diag, far_w, gate, up)

    factor = 2.0 / slots
    hess_shape = S((1, wide, full), F32)
    block = wide * wide * 4
    far_h = chips(hidden)
    pair_h = lax.all_gather(hidden, "tp", axis=0, tiled=True, axis_index_groups=[[0, 1], [2, 3]])
    flip, hidden, hess = call(
        functools.partial(hess_near_kernel, factor, capacity),
        (S((wide, slots), BF16), S((1, slots, wide), BF16), hess_shape),
        [VMEM] * 2, (VMEM, ANY, ANY), (V((2, wide, wide), F32), D((2, 4)), D((8,))), name="hess_near",
        flops=4 * slots * wide * wide, moved=2 * block,
    )(hidden, pair_h)

    def other(which, h, hess):
        return call(
            functools.partial(hess_far_kernel, factor, which), hess_shape,
            [VMEM, VMEM, ANY], ANY, (V((wide, wide), F32), D((4,))), name="hess_%d" % which, aliases={2: 0},
            flops=2 * slots * wide * wide, moved=block,
        )(flip, h, hess)

    far_h = tie(far_h, flip)
    diag_h = cores(far_h)
    hess = other(2, far_h, hess)
    hess = other(3, diag_h, hess)
    return hidden, hess


def general(tokens, expert_ids, gate_weight, up_weight):
    groups = lax.axis_size("ep")
    capacity = 2 * tokens.shape[0] * TOP // EXPERTS
    slots = groups * capacity
    member = jnp.any(expert_ids[:, :, None] == jnp.arange(groups, dtype=jnp.int32), axis=1).astype(jnp.int32)
    rank = jnp.cumsum(member, axis=0) - 1
    chosen = (member.T[:, None, :] > 0) & (rank.T[:, None, :] == jnp.arange(capacity, dtype=jnp.int32)[None, :, None])
    outgoing = jnp.einsum("gcj,jf->gcf", chosen.astype(BF16), tokens, preferred_element_type=F32).astype(BF16)
    arrived = lax.all_to_all(outgoing, "ep", split_axis=0, concat_axis=0, tiled=True)
    routed = lax.all_gather(arrived.reshape(slots, arrived.shape[2]), "tp", axis=1, tiled=True)
    gate = dot(routed, gate_weight[0])
    hidden = (jax.nn.silu(gate) * dot(routed, up_weight[0])).astype(BF16)
    whole = lax.all_gather(hidden, "tp", axis=1, tiled=True)
    hess = lax.dot_general(hidden, whole, (((0,), (0,)), ((), ())), preferred_element_type=F32) * (2.0 / slots)
    return hidden[None], hess[None]


def solution(mesh):
    body = paired if (mesh.shape["ep"], mesh.shape["tp"]) == (8, 4) else general
    return jax.shard_map(
        body,
        mesh=mesh,
        in_specs=(P("ep", "tp"), P("ep", None), P("ep", None, "tp"), P("ep", None, "tp")),
        out_specs=(P("ep", None, "tp"), P("ep", "tp", None)),
        check_vma=False,
    )
```

```python
import functools

import jax
import jax.numpy as jnp
from jax import lax
from jax.experimental import pallas as pl
from jax.experimental.pallas import tpu as pltpu
from jax.sharding import PartitionSpec as P

EXPERTS = 256
TOP = 8
BF16 = jnp.bfloat16
F32 = jnp.float32
VMEM = pl.BlockSpec(memory_space=pltpu.VMEM)
ANY = pl.BlockSpec(memory_space=pl.ANY)
HBM = pl.BlockSpec(memory_space=pltpu.HBM)
LIMIT = 40 * 1024 * 1024


DISTANCE = ((4, 5, 2), (7, 6, 3))
EARLY_ROWS = 512
PARTS = ((1, 2), (0,), (3,))
ORDER = sum(PARTS, ())


def distance(core, k):
    return jnp.where(core == 0, DISTANCE[0][k], DISTANCE[1][k])


def dot(a, b):
    return lax.dot_general(a, b, (((1,), (0,)), ((), ())), preferred_element_type=F32)


def weight_copies(gate_hbm, up_hbm, w_ref, sems, chip, first=0):
    rows = w_ref.shape[1]
    depth = gate_hbm.shape[1] // 2
    at = pl.ds(pl.multiple_of(((lax.axis_index("tp") >> 1) ^ chip) * depth + first, 16), rows)
    return [
        pltpu.make_async_copy(w.at[0, at, :], w_ref.at[i], sems.at[i])
        for i, w in enumerate((gate_hbm, up_hbm))
    ]


def prepare_kernel(capacity, ids_hbm, tok_hbm, gate_hbm, up_hbm, pick_ref, mine_ref, stay_ref, side_ref, w_ref, ids_ref, tok_ref, sems, w_sems):
    get = [
        pltpu.make_async_copy(ids_hbm, ids_ref, sems.at[0]),
        pltpu.make_async_copy(tok_hbm, tok_ref, sems.at[1]),
    ] + weight_copies(gate_hbm, up_hbm, w_ref, w_sems, 0)
    for g in get:
        g.start()
    rows = ids_ref.shape[1]
    before = lax.broadcasted_iota(jnp.int32, (rows, rows), 0)
    after = lax.broadcasted_iota(jnp.int32, (rows, rows), 1)
    upto = jnp.where(before <= after, 1.0, 0.0).astype(BF16)
    want = lax.broadcasted_iota(jnp.int32, (5, capacity, rows), 1).astype(F32)
    core = lax.axis_index("tp") & 1
    step = lax.broadcasted_iota(jnp.int32, (8, rows), 0)
    offset = sum(jnp.where(step == k + 2, distance(core, k), 0) for k in range(3)) + jnp.where(step == 1, 1, 0)
    expert = lax.axis_index("ep") ^ offset
    get[0].wait()
    ids = ids_ref[...]
    hit = ids[0:1, :] == expert
    for k in range(1, ids.shape[0]):
        hit = hit | (ids[k : k + 1, :] == expert)
    count = dot(jnp.where(hit, 1.0, 0.0).astype(BF16), upto)
    slot = jnp.where(hit, count - 1.0, -1.0)[:5]
    pick = jnp.where(slot[:, None, :] == want, 1.0, 0.0)
    pick = pick.reshape(5 * capacity, rows).astype(BF16)
    pick_ref[...] = pick[2 * capacity :]
    get[1].wait()
    taken = dot(pick, tok_ref[...]).astype(BF16)
    stay_ref[...] = taken[:capacity]
    side_ref[...] = taken[capacity : 2 * capacity]
    mine_ref[...] = taken[2 * capacity :]
    get[2].wait()
    get[3].wait()


def select_kernel(capacity, pick_ref, mine_ref, sib_ref, *outs):
    core = lax.axis_index("tp") & 1
    depth = sib_ref.shape[1]
    here = pl.ds(pl.multiple_of(core * depth, depth), depth)
    there = pl.ds(pl.multiple_of((1 - core) * depth, depth), depth)
    other = dot(pick_ref[...], sib_ref[...]).astype(BF16)
    for k, out in enumerate(outs):
        rows = slice(k * capacity, (k + 1) * capacity)
        out[:, here] = mine_ref[rows, :]
        out[:, there] = other[rows]


def load_kernel(after_ref, gate_hbm, up_hbm, near_ref, far_ref, near_sems, far_sems):
    get = weight_copies(gate_hbm, up_hbm, near_ref, near_sems, 0, EARLY_ROWS) + weight_copies(gate_hbm, up_hbm, far_ref, far_sems, 1)
    for g in get:
        g.start()
    for g in get:
        g.wait()


def assemble(capacity, one_ref, other_ref, x_ref):
    core = lax.axis_index("tp") & 1
    depth = x_ref.shape[1] // 2
    for c, ref in ((core, one_ref), (1 - core, other_ref)):
        lanes = pl.ds(pl.multiple_of(c * depth, depth), depth)
        for at, k in enumerate(ORDER):
            block = ref[pl.ds(at * capacity, capacity), :]
            if k == 0:
                x_ref[pl.ds(0, capacity), lanes] = block[:, :depth]
                x_ref[pl.ds(capacity, capacity), lanes] = block[:, depth:]
            else:
                x_ref[pl.ds(pl.multiple_of(distance(c, k - 1) * capacity, capacity), capacity), :] = block


def near_kernel(capacity, own_ref, sib_ref, early_ref, w_ref, g_ref, u_ref, x_ref):
    assemble(capacity, own_ref, sib_ref, x_ref)
    cut = early_ref.shape[1]
    for i, out in enumerate((g_ref, u_ref)):
        out[...] = dot(x_ref[:, :cut], early_ref[i]) + dot(x_ref[:, cut:], w_ref[i])


def far_kernel(capacity, far_ref, diag_ref, w_ref, g_ref, u_ref, h_ref, x_ref):
    assemble(capacity, far_ref, diag_ref, x_ref)
    gate = g_ref[...] + dot(x_ref[...], w_ref[0])
    up = u_ref[...] + dot(x_ref[...], w_ref[1])
    h_ref[...] = (gate / (1.0 + jnp.exp(-gate)) * up).astype(BF16)


def write_block(flip, h, factor, index, hess_hbm, buf, sems):
    wide = h.shape[1]
    part = wide // 4
    at = pl.ds(pl.multiple_of(index * wide, wide), wide)
    copies = []
    for i in range(4):
        rows = pl.ds(i * part, part)
        buf[rows, :] = dot(flip[rows, :], h) * factor
        copies.append(pltpu.make_async_copy(buf.at[rows, :], hess_hbm.at[0, rows, at], sems.at[i]))
        copies[-1].start()
    return copies


def hess_near_kernel(factor, capacity, h_ref, sib_ref, flip_ref, hid_hbm, hess_hbm, buf, sems, out_sems):
    t = lax.axis_index("tp")
    e = lax.axis_index("ep")
    copies = []
    for o in range(8):
        src = h_ref.at[pl.ds(o * capacity, capacity), :]
        at = pl.ds(pl.multiple_of((e ^ o) * capacity, capacity), capacity)
        copies.append(pltpu.make_async_copy(src, hid_hbm.at[0, at, :], out_sems.at[o]))
        copies[-1].start()
    slots = h_ref.shape[0]
    flip_ref[...] = h_ref[...].astype(F32).T.astype(BF16)
    copies += write_block(flip_ref, h_ref[...], factor, t, hess_hbm, buf.at[0], sems.at[0])
    copies += write_block(flip_ref, sib_ref[pl.ds(pl.multiple_of((1 - (t & 1)) * slots, slots), slots), :], factor, t ^ 1, hess_hbm, buf.at[1], sems.at[1])
    for c in copies:
        c.wait()


def hess_far_kernel(factor, which, flip_ref, h_ref, hess_in, hess_hbm, buf, sems):
    t = lax.axis_index("tp")
    for c in write_block(flip_ref, h_ref[...], factor, t ^ which, hess_hbm, buf, sems):
        c.wait()


def call(kernel, out_shape, in_specs, out_specs, scratch=(), name=None, aliases={}, flops=0, moved=0, limit=LIMIT):
    return pl.pallas_call(
        kernel,
        out_shape=out_shape,
        in_specs=in_specs,
        out_specs=out_specs,
        scratch_shapes=list(scratch),
        input_output_aliases=aliases,
        name=name,
        cost_estimate=pl.CostEstimate(flops=flops, bytes_accessed=moved, transcendentals=0),
        compiler_params=pltpu.CompilerParams(vmem_limit_bytes=limit),
    )


def tie(x, after):
    return lax.optimization_barrier((x, after))[0]


def paired(tokens, expert_ids, gate_weight, up_weight):
    groups = 8
    tok_rows, depth = tokens.shape
    capacity = 2 * tok_rows * TOP // EXPERTS
    slots = groups * capacity
    wide = gate_weight.shape[2]
    full = wide * 4
    S = jax.ShapeDtypeStruct
    D = pltpu.SemaphoreType.DMA
    V = pltpu.VMEM

    def chips(x):
        return lax.ppermute(x, "tp", [(i, i ^ 2) for i in range(4)])

    def cores(x):
        return lax.ppermute(x, "tp", [(i, i ^ 1) for i in range(4)])

    def spread(k, x, other_chip=0):
        pairs = [(e * 4 + t, (e ^ DISTANCE[t & 1][k]) * 4 + (t ^ other_chip)) for e in range(8) for t in range(4)]
        return lax.ppermute(x, ("ep", "tp"), pairs)

    sib_tokens = cores(tokens)
    weights = 4 * 2 * depth * 2 * wide
    ids, toks, gate_w, up_w = (
        pltpu.with_memory_space_constraint(a, pltpu.HBM) for a in (expert_ids.T, tokens, gate_weight, up_weight)
    )
    single = S((capacity, depth), BF16)
    half_w = V((2, 2 * depth, wide), BF16)
    early_w = V((2, EARLY_ROWS, wide), BF16)
    rest_w = V((2, 2 * depth - EARLY_ROWS, wide), BF16)
    pick, mine, stay, side, early_w = call(
        functools.partial(prepare_kernel, capacity),
        (S((3 * capacity, tok_rows), BF16), S((3 * capacity, depth), BF16), single, single, early_w),
        [HBM] * 4, (VMEM,) * 5,
        (V(ids.shape, jnp.int32), V(tokens.shape, BF16), D((2,)), D((2,))), name="prepare",
        flops=10 * capacity * tok_rows * depth, moved=tokens.size * 2,
    )(ids, toks, gate_w, up_w)
    side = lax.ppermute(side, "ep", [(e, e ^ 1) for e in range(8)])
    out = call(
        functools.partial(select_kernel, capacity),
        (S((capacity, 2 * depth), BF16),) * 3, [VMEM] * 3, (VMEM,) * 3, name="select",
        flops=6 * capacity * tok_rows * depth,
    )(pick, mine, sib_tokens)
    got = [jnp.concatenate([stay, side], axis=1)] + [spread(k, out[k]) for k in range(3)]
    part = S((slots, wide), F32)
    work = 4 * slots * depth * 2 * wide
    parts = [jnp.concatenate([got[k] for k in part]) for part in PARTS]
    far = jnp.concatenate([chips(part) for part in parts[:-1]] + [spread(k - 1, out[k - 1], 2) for k in PARTS[-1]])
    own = jnp.concatenate(parts)
    sib = cores(own)
    near_w, far_w = call(
        load_kernel, (rest_w, half_w), [VMEM] + [HBM] * 2, (VMEM,) * 2, (D((2,)), D((2,))), name="load", moved=weights,
    )(jnp.concatenate(parts[:2]), gate_w, up_w)
    early = 2 * capacity
    late = tie(far[early:], far_w)
    diag = jnp.concatenate([cores(far[:early]), cores(late)])
    far = jnp.concatenate([far[:early], late])
    x = V((slots, 2 * depth), BF16)
    gate, up = call(
        functools.partial(near_kernel, capacity), (part, part), [VMEM] * 4, (VMEM,) * 2, (x,), name="near",
        flops=work, moved=weights // 2,
    )(own, tie(sib, far), early_w, near_w)
    hidden = call(
        functools.partial(far_kernel, capacity), S((slots, wide), BF16), [VMEM] * 5, VMEM, (x,), name="far",
        flops=work, moved=weights // 2,
    )(far, diag, far_w, gate, up)

    factor = 2.0 / slots
    hess_shape = S((1, wide, full), F32)
    block = wide * wide * 4
    far_h = chips(hidden)
    pair_h = lax.all_gather(hidden, "tp", axis=0, tiled=True, axis_index_groups=[[0, 1], [2, 3]])
    flip, hidden, hess = call(
        functools.partial(hess_near_kernel, factor, capacity),
        (S((wide, slots), BF16), S((1, slots, wide), BF16), hess_shape),
        [VMEM] * 2, (VMEM, ANY, ANY), (V((2, wide, wide), F32), D((2, 4)), D((8,))), name="hess_near",
        flops=4 * slots * wide * wide, moved=2 * block,
    )(hidden, pair_h)

    def other(which, h, hess):
        return call(
            functools.partial(hess_far_kernel, factor, which), hess_shape,
            [VMEM, VMEM, ANY], ANY, (V((wide, wide), F32), D((4,))), name="hess_%d" % which, aliases={2: 0},
            flops=2 * slots * wide * wide, moved=block,
        )(flip, h, hess)

    far_h = tie(far_h, flip)
    diag_h = cores(far_h)
    hess = other(2, far_h, hess)
    hess = other(3, diag_h, hess)
    return hidden, hess


def general(tokens, expert_ids, gate_weight, up_weight):
    groups = lax.axis_size("ep")
    capacity = 2 * tokens.shape[0] * TOP // EXPERTS
    slots = groups * capacity
    member = jnp.any(expert_ids[:, :, None] == jnp.arange(groups, dtype=jnp.int32), axis=1).astype(jnp.int32)
    rank = jnp.cumsum(member, axis=0) - 1
    chosen = (member.T[:, None, :] > 0) & (rank.T[:, None, :] == jnp.arange(capacity, dtype=jnp.int32)[None, :, None])
    outgoing = jnp.einsum("gcj,jf->gcf", chosen.astype(BF16), tokens, preferred_element_type=F32).astype(BF16)
    arrived = lax.all_to_all(outgoing, "ep", split_axis=0, concat_axis=0, tiled=True)
    routed = lax.all_gather(arrived.reshape(slots, arrived.shape[2]), "tp", axis=1, tiled=True)
    gate = dot(routed, gate_weight[0])
    hidden = (jax.nn.silu(gate) * dot(routed, up_weight[0])).astype(BF16)
    whole = lax.all_gather(hidden, "tp", axis=1, tiled=True)
    hess = lax.dot_general(hidden, whole, (((0,), (0,)), ((), ())), preferred_element_type=F32) * (2.0 / slots)
    return hidden[None], hess[None]


def solution(mesh):
    body = paired if (mesh.shape["ep"], mesh.shape["tp"]) == (8, 4) else general
    return jax.shard_map(
        body,
        mesh=mesh,
        in_specs=(P("ep", "tp"), P("ep", None), P("ep", None, "tp"), P("ep", None, "tp")),
        out_specs=(P("ep", None, "tp"), P("ep", "tp", None)),
        check_vma=False,
    )
```

```python
import functools

import jax
import jax.numpy as jnp
from jax import lax
from jax.experimental import pallas as pl
from jax.experimental.pallas import tpu as pltpu
from jax.sharding import PartitionSpec as P

EXPERTS = 256
TOP = 8
BF16 = jnp.bfloat16
F32 = jnp.float32
VMEM = pl.BlockSpec(memory_space=pltpu.VMEM)
ANY = pl.BlockSpec(memory_space=pl.ANY)
HBM = pl.BlockSpec(memory_space=pltpu.HBM)
LIMIT = 40 * 1024 * 1024


DISTANCE = ((5, 6, 2), (4, 7, 3))
EARLY_ROWS = 384
PARTS = ((1, 2), (0,), (3,))
ORDER = sum(PARTS, ())


def distance(core, k):
    return jnp.where(core == 0, DISTANCE[0][k], DISTANCE[1][k])


def dot(a, b):
    return lax.dot_general(a, b, (((1,), (0,)), ((), ())), preferred_element_type=F32)


def weight_copies(gate_hbm, up_hbm, w_ref, sems, chip, first=0):
    rows = w_ref.shape[1]
    depth = gate_hbm.shape[1] // 2
    at = pl.ds(pl.multiple_of(((lax.axis_index("tp") >> 1) ^ chip) * depth + first, 16), rows)
    return [
        pltpu.make_async_copy(w.at[0, at, :], w_ref.at[i], sems.at[i])
        for i, w in enumerate((gate_hbm, up_hbm))
    ]


def prepare_kernel(capacity, ids_hbm, tok_hbm, gate_hbm, up_hbm, pick_ref, mine_ref, stay_ref, side_ref, w_ref, ids_ref, tok_ref, sems, w_sems):
    get = [
        pltpu.make_async_copy(ids_hbm, ids_ref, sems.at[0]),
        pltpu.make_async_copy(tok_hbm, tok_ref, sems.at[1]),
    ] + weight_copies(gate_hbm, up_hbm, w_ref, w_sems, 0)
    for g in get:
        g.start()
    rows = ids_ref.shape[1]
    before = lax.broadcasted_iota(jnp.int32, (rows, rows), 0)
    after = lax.broadcasted_iota(jnp.int32, (rows, rows), 1)
    upto = jnp.where(before <= after, 1.0, 0.0).astype(BF16)
    want = lax.broadcasted_iota(jnp.int32, (5, capacity, rows), 1).astype(F32)
    core = lax.axis_index("tp") & 1
    step = lax.broadcasted_iota(jnp.int32, (8, rows), 0)
    offset = sum(jnp.where(step == k + 2, distance(core, k), 0) for k in range(3)) + jnp.where(step == 1, 1, 0)
    expert = lax.axis_index("ep") ^ offset
    get[0].wait()
    ids = ids_ref[...]
    hit = ids[0:1, :] == expert
    for k in range(1, ids.shape[0]):
        hit = hit | (ids[k : k + 1, :] == expert)
    count = dot(jnp.where(hit, 1.0, 0.0).astype(BF16), upto)
    slot = jnp.where(hit, count - 1.0, -1.0)[:5]
    pick = jnp.where(slot[:, None, :] == want, 1.0, 0.0)
    pick = pick.reshape(5 * capacity, rows).astype(BF16)
    pick_ref[...] = pick[2 * capacity :]
    get[1].wait()
    taken = dot(pick, tok_ref[...]).astype(BF16)
    stay_ref[...] = taken[:capacity]
    side_ref[...] = taken[capacity : 2 * capacity]
    mine_ref[...] = taken[2 * capacity :]
    get[2].wait()
    get[3].wait()


def select_kernel(capacity, pick_ref, mine_ref, sib_ref, *outs):
    core = lax.axis_index("tp") & 1
    depth = sib_ref.shape[1]
    here = pl.ds(pl.multiple_of(core * depth, depth), depth)
    there = pl.ds(pl.multiple_of((1 - core) * depth, depth), depth)
    other = dot(pick_ref[...], sib_ref[...]).astype(BF16)
    for k, out in enumerate(outs):
        rows = slice(k * capacity, (k + 1) * capacity)
        out[:, here] = mine_ref[rows, :]
        out[:, there] = other[rows]


def load_kernel(after_ref, gate_hbm, up_hbm, near_ref, far_ref, near_sems, far_sems):
    get = weight_copies(gate_hbm, up_hbm, near_ref, near_sems, 0, EARLY_ROWS) + weight_copies(gate_hbm, up_hbm, far_ref, far_sems, 1)
    for g in get:
        g.start()
    for g in get:
        g.wait()


def assemble(capacity, one_ref, other_ref, x_ref):
    core = lax.axis_index("tp") & 1
    depth = x_ref.shape[1] // 2
    for c, ref in ((core, one_ref), (1 - core, other_ref)):
        lanes = pl.ds(pl.multiple_of(c * depth, depth), depth)
        for at, k in enumerate(ORDER):
            block = ref[pl.ds(at * capacity, capacity), :]
            if k == 0:
                x_ref[pl.ds(0, capacity), lanes] = block[:, :depth]
                x_ref[pl.ds(capacity, capacity), lanes] = block[:, depth:]
            else:
                x_ref[pl.ds(pl.multiple_of(distance(c, k - 1) * capacity, capacity), capacity), :] = block


def near_kernel(capacity, own_ref, sib_ref, early_ref, w_ref, g_ref, u_ref, x_ref):
    assemble(capacity, own_ref, sib_ref, x_ref)
    cut = early_ref.shape[1]
    for i, out in enumerate((g_ref, u_ref)):
        out[...] = dot(x_ref[:, :cut], early_ref[i]) + dot(x_ref[:, cut:], w_ref[i])


def far_kernel(capacity, far_ref, diag_ref, w_ref, g_ref, u_ref, h_ref, x_ref):
    assemble(capacity, far_ref, diag_ref, x_ref)
    gate = g_ref[...] + dot(x_ref[...], w_ref[0])
    up = u_ref[...] + dot(x_ref[...], w_ref[1])
    h_ref[...] = (gate / (1.0 + jnp.exp(-gate)) * up).astype(BF16)


def write_block(flip, h, factor, index, hess_hbm, buf, sems):
    wide = h.shape[1]
    part = wide // 4
    at = pl.ds(pl.multiple_of(index * wide, wide), wide)
    copies = []
    for i in range(4):
        rows = pl.ds(i * part, part)
        buf[rows, :] = dot(flip[rows, :], h) * factor
        copies.append(pltpu.make_async_copy(buf.at[rows, :], hess_hbm.at[0, rows, at], sems.at[i]))
        copies[-1].start()
    return copies


def hess_near_kernel(factor, capacity, h_ref, sib_ref, flip_ref, hid_hbm, hess_hbm, buf, sems, out_sems):
    t = lax.axis_index("tp")
    e = lax.axis_index("ep")
    copies = []
    for o in range(8):
        src = h_ref.at[pl.ds(o * capacity, capacity), :]
        at = pl.ds(pl.multiple_of((e ^ o) * capacity, capacity), capacity)
        copies.append(pltpu.make_async_copy(src, hid_hbm.at[0, at, :], out_sems.at[o]))
        copies[-1].start()
    slots = h_ref.shape[0]
    flip_ref[...] = h_ref[...].astype(F32).T.astype(BF16)
    copies += write_block(flip_ref, h_ref[...], factor, t, hess_hbm, buf.at[0], sems.at[0])
    copies += write_block(flip_ref, sib_ref[pl.ds(pl.multiple_of((1 - (t & 1)) * slots, slots), slots), :], factor, t ^ 1, hess_hbm, buf.at[1], sems.at[1])
    for c in copies:
        c.wait()


def hess_far_kernel(factor, which, flip_ref, h_ref, hess_in, hess_hbm, buf, sems):
    t = lax.axis_index("tp")
    for c in write_block(flip_ref, h_ref[...], factor, t ^ which, hess_hbm, buf, sems):
        c.wait()


def call(kernel, out_shape, in_specs, out_specs, scratch=(), name=None, aliases={}, flops=0, moved=0, limit=LIMIT):
    return pl.pallas_call(
        kernel,
        out_shape=out_shape,
        in_specs=in_specs,
        out_specs=out_specs,
        scratch_shapes=list(scratch),
        input_output_aliases=aliases,
        name=name,
        cost_estimate=pl.CostEstimate(flops=flops, bytes_accessed=moved, transcendentals=0),
        compiler_params=pltpu.CompilerParams(vmem_limit_bytes=limit),
    )


def tie(x, after):
    return lax.optimization_barrier((x, after))[0]


def paired(tokens, expert_ids, gate_weight, up_weight):
    groups = 8
    tok_rows, depth = tokens.shape
    capacity = 2 * tok_rows * TOP // EXPERTS
    slots = groups * capacity
    wide = gate_weight.shape[2]
    full = wide * 4
    S = jax.ShapeDtypeStruct
    D = pltpu.SemaphoreType.DMA
    V = pltpu.VMEM

    def chips(x):
        return lax.ppermute(x, "tp", [(i, i ^ 2) for i in range(4)])

    def cores(x):
        return lax.ppermute(x, "tp", [(i, i ^ 1) for i in range(4)])

    def spread(k, x, other_chip=0):
        pairs = [(e * 4 + t, (e ^ DISTANCE[t & 1][k]) * 4 + (t ^ other_chip)) for e in range(8) for t in range(4)]
        return lax.ppermute(x, ("ep", "tp"), pairs)

    sib_tokens = cores(tokens)
    weights = 4 * 2 * depth * 2 * wide
    ids, toks, gate_w, up_w = (
        pltpu.with_memory_space_constraint(a, pltpu.HBM) for a in (expert_ids.T, tokens, gate_weight, up_weight)
    )
    single = S((capacity, depth), BF16)
    half_w = V((2, 2 * depth, wide), BF16)
    early_w = V((2, EARLY_ROWS, wide), BF16)
    rest_w = V((2, 2 * depth - EARLY_ROWS, wide), BF16)
    pick, mine, stay, side, early_w = call(
        functools.partial(prepare_kernel, capacity),
        (S((3 * capacity, tok_rows), BF16), S((3 * capacity, depth), BF16), single, single, early_w),
        [HBM] * 4, (VMEM,) * 5,
        (V(ids.shape, jnp.int32), V(tokens.shape, BF16), D((2,)), D((2,))), name="prepare",
        flops=10 * capacity * tok_rows * depth, moved=tokens.size * 2,
    )(ids, toks, gate_w, up_w)
    side = lax.ppermute(side, "ep", [(e, e ^ 1) for e in range(8)])
    out = call(
        functools.partial(select_kernel, capacity),
        (S((capacity, 2 * depth), BF16),) * 3, [VMEM] * 3, (VMEM,) * 3, name="select",
        flops=6 * capacity * tok_rows * depth,
    )(pick, mine, sib_tokens)
    got = [jnp.concatenate([stay, side], axis=1)] + [spread(k, out[k]) for k in range(3)]
    part = S((slots, wide), F32)
    work = 4 * slots * depth * 2 * wide
    parts = [jnp.concatenate([got[k] for k in part]) for part in PARTS]
    far = jnp.concatenate([chips(part) for part in parts[:-1]] + [spread(k - 1, out[k - 1], 2) for k in PARTS[-1]])
    own = jnp.concatenate(parts)
    sib = cores(own)
    near_w, far_w = call(
        load_kernel, (rest_w, half_w), [VMEM] + [HBM] * 2, (VMEM,) * 2, (D((2,)), D((2,))), name="load", moved=weights,
    )(jnp.concatenate(parts[:2]), gate_w, up_w)
    early = 2 * capacity
    late = tie(far[early:], far_w)
    diag = jnp.concatenate([cores(far[:early]), cores(late)])
    far = jnp.concatenate([far[:early], late])
    x = V((slots, 2 * depth), BF16)
    gate, up = call(
        functools.partial(near_kernel, capacity), (part, part), [VMEM] * 4, (VMEM,) * 2, (x,), name="near",
        flops=work, moved=weights // 2,
    )(own, tie(sib, far), early_w, near_w)
    hidden = call(
        functools.partial(far_kernel, capacity), S((slots, wide), BF16), [VMEM] * 5, VMEM, (x,), name="far",
        flops=work, moved=weights // 2,
    )(far, diag, far_w, gate, up)

    factor = 2.0 / slots
    hess_shape = S((1, wide, full), F32)
    block = wide * wide * 4
    far_h = chips(hidden)
    pair_h = lax.all_gather(hidden, "tp", axis=0, tiled=True, axis_index_groups=[[0, 1], [2, 3]])
    flip, hidden, hess = call(
        functools.partial(hess_near_kernel, factor, capacity),
        (S((wide, slots), BF16), S((1, slots, wide), BF16), hess_shape),
        [VMEM] * 2, (VMEM, ANY, ANY), (V((2, wide, wide), F32), D((2, 4)), D((8,))), name="hess_near",
        flops=4 * slots * wide * wide, moved=2 * block,
    )(hidden, pair_h)

    def other(which, h, hess):
        return call(
            functools.partial(hess_far_kernel, factor, which), hess_shape,
            [VMEM, VMEM, ANY], ANY, (V((wide, wide), F32), D((4,))), name="hess_%d" % which, aliases={2: 0},
            flops=2 * slots * wide * wide, moved=block,
        )(flip, h, hess)

    far_h = tie(far_h, flip)
    diag_h = cores(far_h)
    hess = other(2, far_h, hess)
    hess = other(3, diag_h, hess)
    return hidden, hess


def general(tokens, expert_ids, gate_weight, up_weight):
    groups = lax.axis_size("ep")
    capacity = 2 * tokens.shape[0] * TOP // EXPERTS
    slots = groups * capacity
    member = jnp.any(expert_ids[:, :, None] == jnp.arange(groups, dtype=jnp.int32), axis=1).astype(jnp.int32)
    rank = jnp.cumsum(member, axis=0) - 1
    chosen = (member.T[:, None, :] > 0) & (rank.T[:, None, :] == jnp.arange(capacity, dtype=jnp.int32)[None, :, None])
    outgoing = jnp.einsum("gcj,jf->gcf", chosen.astype(BF16), tokens, preferred_element_type=F32).astype(BF16)
    arrived = lax.all_to_all(outgoing, "ep", split_axis=0, concat_axis=0, tiled=True)
    routed = lax.all_gather(arrived.reshape(slots, arrived.shape[2]), "tp", axis=1, tiled=True)
    gate = dot(routed, gate_weight[0])
    hidden = (jax.nn.silu(gate) * dot(routed, up_weight[0])).astype(BF16)
    whole = lax.all_gather(hidden, "tp", axis=1, tiled=True)
    hess = lax.dot_general(hidden, whole, (((0,), (0,)), ((), ())), preferred_element_type=F32) * (2.0 / slots)
    return hidden[None], hess[None]


def solution(mesh):
    body = paired if (mesh.shape["ep"], mesh.shape["tp"]) == (8, 4) else general
    return jax.shard_map(
        body,
        mesh=mesh,
        in_specs=(P("ep", "tp"), P("ep", None), P("ep", None, "tp"), P("ep", None, "tp")),
        out_specs=(P("ep", None, "tp"), P("ep", "tp", None)),
        check_vma=False,
    )
```
